256 devices in a mesh: dp: 16 (over z_lo, y), ctx: 16 (over x, z_hi, core).
Axes of the slice: x: 4, y: 4, z: 8 (z_hi: 2, z_lo: 4; z = z_hi * 4 + z_lo), core: 2. Of those that a mesh axis runs over, the one named last changes fastest.
Arguments:
- queries: bfloat16 [2, 16, 2048, 2560], P(None, 'dp', 'ctx'), may hold values from -100 to 100
- keys_values: bfloat16 [16, 2048, 1024], P('dp', 'ctx'), may hold values from -5 to 5
- grad_out: bfloat16 [2, 16, 2048, 2560], P(None, 'dp', 'ctx'), may hold values from -6 to 6
- hidden_kv: bfloat16 [16, 2048, 5120], P(None, 'ctx', 'dp'), may hold values from -6 to 6
- doc_lengths: int32 [16, 16], P('dp'), may hold values from 1 to 256, 2048 in all within a row
Outputs:
- query_grad: bfloat16 [2, 16, 2048, 2560], P(None, 'dp', 'ctx')
- key_value_grad: bfloat16 [16, 2048, 1024], P('dp', 'ctx')
- weight_grad: float32 [5120, 1024], P(('dp', 'ctx'))
The draws below stay inside these ranges and needn't reach their ends.
All inputs are finite; a program needn't handle non-finite values.
Results may differ from the reference program's by a relative error of at most 0.0077.
Values may be sent and summed in bfloat16 or wider, within the bound.
No kernel may reach another device: no remote copies, remote signals or barrier semaphores. Data moves between devices by JAX's collectives and lax.ppermute only.
A program may use at most 64 MiB of HBM per device.

```python
import math
import jax
import jax.numpy as jnp
import numpy as np
from jax import lax

D = 5120
KV_HEADS = 4
GROUP = 5
HEAD_DIM = 128
HEADS = 20
LAYERS = 2
REACH = 2
TOK_DEV = 128
SEQ = 2048
MOST = 256
DOCS = 16
N_DP = 16
N_CTX = 16


def shared_keys(key):
    return jnp.clip(jax.random.normal(key, (N_DP, SEQ, KV_HEADS * HEAD_DIM), jnp.float32), -5.0, 5.0)


def draw_keys_values(key, part):
    keys_raw = shared_keys(key)
    key = jax.random.fold_in(key, 11)
    values = jnp.clip(jax.random.normal(key, (N_DP, SEQ, KV_HEADS * HEAD_DIM), jnp.float32), -5.0, 5.0)
    return jnp.concatenate([keys_raw, values], axis=-1).astype(jnp.bfloat16)


def draw_queries(key, part):
    key = jax.random.fold_in(key, 12)
    base = jnp.clip(jax.random.normal(key, (LAYERS, N_DP, SEQ, HEADS * HEAD_DIM), jnp.float32), -5.0, 5.0)
    return base.astype(jnp.bfloat16)


def level_of(rng, dims, cuts, least, top_value):
    level, own = 1.0, jax.random.fold_in(rng, 6)
    for position, shards_of in cuts:
        steps = jnp.exp(jax.random.uniform(jax.random.fold_in(own, position), (shards_of,), jnp.float32, least / len(cuts), top_value / len(cuts)))
        level = level * jnp.repeat(steps, dims[position] // shards_of).reshape([-1 if axis == position else 1 for axis in range(len(dims))])
    return level


def split_up(number_of, total, reach, slope):
    loads = [(1 << 20) // math.isqrt(standing ** slope) + 1 for standing in range(2, number_of + 1)]
    spare, counts = total - reach - (number_of - 1), [1] * (number_of - 1)
    while spare > 0:
        candidates = [i for i in range(number_of - 1) if counts[i] < reach]
        mass, left = sum([loads[i] for i in candidates]), spare
        for i in candidates:
            extra = min(reach - counts[i], max(1, left * loads[i] // mass), spare)
            counts[i] = counts[i] + extra
            spare = spare - extra
    return np.array([reach] + counts)


def ragged(stream_key, count, total, limit, lean):
    if count == 2:
        one = jax.random.randint(stream_key, (), max(1, total - limit), min(limit, total - 1) + 1)
        return jnp.stack([one, total - one])
    sizes = jnp.asarray(split_up(count, total, limit, lean), jnp.int32)
    twos = (count - 1) // 2
    source_of, receiver = sizes[1:1 + 2 * twos:2], sizes[2:2 + 2 * twos:2]
    slack = jnp.minimum(source_of - 1, limit - receiver)
    moved = jax.random.randint(jax.random.fold_in(stream_key, 1), (twos,), 0, 1 << 20) % (slack + 1)
    sizes = sizes.at[1:1 + 2 * twos:2].set(source_of - moved).at[2:2 + 2 * twos:2].set(receiver + moved)
    return sizes[jax.random.permutation(jax.random.fold_in(stream_key, 2), count)]


def centred(stream_key, dims, scale, limit, pieces=(), kind=jnp.bfloat16):
    result = scale * jax.random.normal(stream_key, dims, jnp.float32)
    if pieces:
        result = result * level_of(stream_key, dims, pieces, -0.22, 0.18)
    return jnp.clip(result, -limit, limit).astype(kind)


def setup_inputs(seed: int = 0) -> dict:
    key_list = jax.random.split(jax.random.key(seed), 6)
    return {
        "queries": draw_queries(jax.random.fold_in(key_list[5], 71), 0),
        "keys_values": draw_keys_values(jax.random.fold_in(key_list[5], 71), 0),
        "grad_out": centred(key_list[2], (LAYERS, N_DP, SEQ, HEADS * HEAD_DIM), 1.0, 6.0, ((1, 16), (2, 16))),
        "hidden_kv": centred(key_list[3], (N_DP, SEQ, D), 1.0, 6.0, ((1, 16), (2, 16))),
        "doc_lengths": jax.vmap(lambda own: ragged(own, DOCS, SEQ, MOST, 2))(jax.random.split(key_list[4], N_DP)).reshape((N_DP, DOCS)).astype(jnp.int32),
    }


def visibility(query_pos, key_pos, lengths):
    ends = jnp.cumsum(lengths).astype(jnp.int32)
    query_doc = lax.optimization_barrier(jnp.sum((query_pos[:, None] >= ends[None, :]).astype(jnp.int32), axis=1))
    key_doc = lax.optimization_barrier(jnp.sum((key_pos[:, None] >= ends[None, :]).astype(jnp.int32), axis=1))
    return (key_pos[None, :] >= 0) & (key_pos[None, :] <= query_pos[:, None]) & (key_doc[None, :] == query_doc[:, None])

def window_grads(q_block, do_block, window, visible):
    tok_rows = q_block.shape[0]
    width = window.shape[0]
    factor = 1.0 / math.sqrt(HEAD_DIM)
    split_at = KV_HEADS * HEAD_DIM
    q_heads = q_block.reshape(tok_rows, KV_HEADS, GROUP, HEAD_DIM).astype(jnp.float32)
    do_heads = do_block.reshape(tok_rows, KV_HEADS, GROUP, HEAD_DIM).astype(jnp.float32)
    keys = window[:, :split_at].reshape(width, KV_HEADS, HEAD_DIM).astype(jnp.float32)
    values = window[:, split_at:].reshape(width, KV_HEADS, HEAD_DIM).astype(jnp.float32)
    scores = jnp.einsum('tkgd,wkd->kgtw', q_heads, keys) * factor
    scores = jnp.where(visible[None, None], scores, -jnp.inf)
    probs = jax.nn.softmax(scores, axis=-1)
    probs_b = lax.optimization_barrier(probs.astype(jnp.bfloat16)).astype(jnp.float32)
    attn = jnp.einsum('kgtw,wkd->tkgd', probs_b, values)
    delta = jnp.einsum('tkgd,tkgd->kgt', do_heads, attn)
    dprobs = jnp.einsum('tkgd,wkd->kgtw', do_heads, values)
    dscores = probs * (dprobs - delta[..., None])
    dscores_b = lax.optimization_barrier(dscores.astype(jnp.bfloat16)).astype(jnp.float32)
    dq = jnp.einsum('kgtw,wkd->tkgd', dscores_b, keys) * factor
    dk = jnp.einsum('kgtw,tkgd->wkd', dscores_b, q_heads) * factor
    dv = jnp.einsum('kgtw,tkgd->wkd', probs_b, do_heads)
    both = jnp.concatenate([dk.reshape(width, split_at), dv.reshape(width, split_at)], axis=1)
    return (dq.reshape(tok_rows, KV_HEADS * GROUP * HEAD_DIM), both)

def one_sequence(q_seq, kv_seq, do_seq, lengths):
    tok_rows = TOK_DEV
    width = (REACH + 1) * tok_rows
    columns = kv_seq.shape[1]
    padded = jnp.concatenate([jnp.zeros((REACH * tok_rows, columns), jnp.bfloat16), kv_seq], axis=0)

    def step(accum, block):
        start = (block * tok_rows).astype(jnp.int32)
        window = lax.dynamic_slice_in_dim(padded, start, width, 0)
        query_pos = start + jnp.arange(tok_rows, dtype=jnp.int32)
        key_pos = start - REACH * tok_rows + jnp.arange(width, dtype=jnp.int32)
        visible = visibility(query_pos, key_pos, lengths)
        grads = []
        for layer in range(LAYERS):
            q_block = lax.dynamic_slice_in_dim(q_seq[layer], start, tok_rows, 0)
            do_block = lax.dynamic_slice_in_dim(do_seq[layer], start, tok_rows, 0)
            dq, both = window_grads(q_block, do_block, window, visible)
            current = lax.dynamic_slice_in_dim(accum, start, width, 0)
            accum = lax.dynamic_update_slice_in_dim(accum, current + both, start, 0)
            grads.append(dq.astype(jnp.bfloat16))
        return (accum, jnp.stack(grads))
    accum, dq_blocks = lax.scan(step, jnp.zeros((SEQ + REACH * tok_rows, columns), jnp.float32), jnp.arange(N_CTX, dtype=jnp.int32))
    dq_seq = dq_blocks.transpose(1, 0, 2, 3).reshape(LAYERS, SEQ, dq_blocks.shape[-1])
    return (dq_seq, accum[REACH * tok_rows:].astype(jnp.bfloat16))

def reference(queries, keys_values, grad_out, hidden_kv, doc_lengths):

    def per_seq(weight_acc, inputs):
        q_seq, kv_seq, do_seq, states, lengths = inputs
        dq_seq, kv_grad = one_sequence(q_seq, kv_seq, do_seq, lengths)
        term = lax.dot_general(states, kv_grad, (((0,), (0,)), ((), ())), preferred_element_type=jnp.float32)
        return (weight_acc + term, (dq_seq, kv_grad))
    weight_grad, (dq_all, kv_all) = lax.scan(per_seq, jnp.zeros((D, keys_values.shape[2]), jnp.float32), (queries.transpose(1, 0, 2, 3), keys_values, grad_out.transpose(1, 0, 2, 3), hidden_kv, doc_lengths))
    return (dq_all.transpose(1, 0, 2, 3), kv_all, weight_grad)
```

```python
import functools
import math

import jax
import jax.numpy as jnp
from jax import lax
from jax.experimental import pallas as pl
from jax.experimental.pallas import tpu as pltpu
from jax.sharding import Mesh, PartitionSpec as P

KV_HEADS = 4
GROUP = 5
HEAD_DIM = 128
LAYERS = 2
TOK = 128
FACTOR = 1.0 / math.sqrt(HEAD_DIM)
AXES = ("zl", "y", "x", "zh", "core")
SIZES = {"zl": 4, "y": 4, "x": 4, "zh": 2, "core": 2}
GATHER = "zl"
SPREAD = "y"


def shift(value, axis, by):
    size = SIZES[axis]
    return lax.ppermute(value, axis, [(i, (i + by) % size) for i in range(size)])


def ctx_shift(value, by):
    pairs = [(i, i + by) for i in range(16) if 0 <= i + by < 16]
    return lax.ppermute(value, ("x", "zh", "core"), pairs)


def attention_kernel(bias_ref, q_ref, do_ref, k0_ref, k1_ref, k2_ref, v0_ref, v1_ref, v2_ref, dq_ref, own_ref, one_ref, two_ref):
    keys = jnp.concatenate([k0_ref[...], k1_ref[...], k2_ref[...]], axis=0)
    values = jnp.concatenate([v0_ref[...], v1_ref[...], v2_ref[...]], axis=0)
    keys_t = keys.T
    bias = jnp.concatenate([bias_ref[...]] * LAYERS, axis=1)
    shape = (TOK, LAYERS * TOK)
    key_at = lax.broadcasted_iota(jnp.int32, shape, 0)
    query_at = lax.broadcasted_iota(jnp.int32, shape, 1) % TOK
    lower = key_at <= query_at
    lower_b = lower.astype(jnp.float32).astype(jnp.bfloat16)
    upper_b = 1 - lower_b
    nt = (((1,), (1,)), ((), ()))
    dk = jnp.zeros((3 * TOK, HEAD_DIM), jnp.float32)
    dv = jnp.zeros((3 * TOK, HEAD_DIM), jnp.float32)
    for g in range(GROUP):
        cols = slice(g * HEAD_DIM, (g + 1) * HEAD_DIM)
        q = jnp.concatenate([q_ref[0, :, cols], q_ref[1, :, cols]], axis=0)
        do = jnp.concatenate([do_ref[0, :, cols], do_ref[1, :, cols]], axis=0)
        s = lax.dot_general(keys, q, nt, preferred_element_type=jnp.float32)
        dp = lax.dot_general(values, do, nt, preferred_element_type=jnp.float32)
        s = jnp.concatenate([jnp.where(lower, s[:TOK], s[2 * TOK :]), s[TOK : 2 * TOK]], axis=0)
        dp = jnp.concatenate([jnp.where(lower, dp[:TOK], dp[2 * TOK :]), dp[TOK : 2 * TOK]], axis=0)
        s = s * (FACTOR * math.log2(math.e)) + bias
        e = jnp.exp2(s - jnp.max(s, axis=0, keepdims=True))
        p = e * (1.0 / jnp.sum(e, axis=0, keepdims=True))
        delta = jnp.sum(p * dp, axis=0, keepdims=True)
        ds = (p * (dp - delta)).astype(jnp.bfloat16)
        p = p.astype(jnp.bfloat16)
        p = jnp.concatenate([p[:TOK] * lower_b, p[TOK:], p[:TOK] * upper_b], axis=0)
        ds = jnp.concatenate([ds[:TOK] * lower_b, ds[TOK:], ds[:TOK] * upper_b], axis=0)
        dv += jnp.dot(p, do, preferred_element_type=jnp.float32)
        dk += jnp.dot(ds, q, preferred_element_type=jnp.float32)
        dq = jnp.dot(keys_t, ds, preferred_element_type=jnp.float32) * FACTOR
        dq = dq.astype(jnp.bfloat16).T
        dq_ref[0, :, cols] = dq[:TOK]
        dq_ref[1, :, cols] = dq[TOK:]
    dk = dk * FACTOR
    both = jnp.concatenate([dk, dv], axis=1)
    own_ref[...] = both[:TOK]
    one_ref[...] = both[TOK : 2 * TOK].astype(jnp.bfloat16)
    two_ref[...] = both[2 * TOK :].astype(jnp.bfloat16)


def attention(bias, queries, grad_out, kv0, kv1, kv2):
    wide = GROUP * HEAD_DIM
    rows = pl.BlockSpec((LAYERS, TOK, wide), lambda h: (0, 0, h))
    key_cols = pl.BlockSpec((TOK, HEAD_DIM), lambda h: (0, h))
    value_cols = pl.BlockSpec((TOK, HEAD_DIM), lambda h: (0, KV_HEADS + h))
    pair = pl.BlockSpec((TOK, 2 * HEAD_DIM), lambda h: (0, h))
    full = (TOK, KV_HEADS * 2 * HEAD_DIM)
    return pl.pallas_call(
        attention_kernel,
        grid=(KV_HEADS,),
        in_specs=[pl.BlockSpec((2 * TOK, TOK), lambda h: (0, 0)), rows, rows] + [key_cols] * 3 + [value_cols] * 3,
        out_specs=[rows, pair, pair, pair],
        out_shape=[
            jax.ShapeDtypeStruct(queries.shape, jnp.bfloat16),
            jax.ShapeDtypeStruct(full, jnp.float32),
            jax.ShapeDtypeStruct(full, jnp.bfloat16),
            jax.ShapeDtypeStruct(full, jnp.bfloat16),
        ],
        compiler_params=pltpu.CompilerParams(vmem_limit_bytes=32 * 1024 * 1024),
        cost_estimate=pl.CostEstimate(flops=6_000_000_000, bytes_accessed=9_000_000, transcendentals=1_400_000),
        name="attention",
    )(bias, queries, grad_out, kv0, kv1, kv2, kv0, kv1, kv2)


def mask_bias(position, lengths):
    ends = jnp.cumsum(lengths)
    own = jnp.arange(TOK, dtype=jnp.int32)

    def doc(pos):
        return jnp.sum((pos[:, None] >= ends[None, :]).astype(jnp.int32), axis=1)

    query_doc = doc(position + own)
    zero, one, two = ((position - back * TOK + own) for back in (0, 1, 2))
    lower = own[:, None] <= own[None, :]
    seen = [(pos >= 0)[:, None] & (doc(pos)[:, None] == query_doc[None, :]) for pos in (zero, one, two)]
    seen = jnp.concatenate([jnp.where(lower, seen[0], seen[2]), seen[1]], axis=0)
    return jnp.where(seen, 0.0, -jnp.inf).astype(jnp.float32)


def pick(value, index, axis):
    return lax.dynamic_index_in_dim(value, index, axis, keepdims=False)


def spread_hidden(hidden):
    me = lax.axis_index(SPREAD)
    parts = hidden.reshape(4, 4, TOK, 320)
    axis = 1 if SPREAD == "y" else 0
    got = [pick(parts, me, axis)]
    for by in (1, 2, 3):
        got.append(shift(pick(parts, (me + by) % 4, axis), SPREAD, by))
    other = [shift(part, "core", 1) for part in got]
    return got, other


def total(parts):
    acc = parts[0].astype(jnp.float32)
    for part in parts[1:]:
        acc = acc + part.astype(jnp.float32)
    return acc


def on_device(queries, keys_values, grad_out, hidden_kv, doc_lengths):
    core = lax.axis_index("core")
    zh = lax.axis_index("zh")
    x = lax.axis_index("x")
    me = lax.axis_index(SPREAD)
    position = ((x * 2 + zh) * 2 + core) * TOK
    kv0 = keys_values[0]
    kv2 = ctx_shift(kv0, 2)
    kv1 = shift(jnp.where(core == 1, kv2, kv0), "core", 1)
    bias = mask_bias(position, doc_lengths[0])
    hidden_own, hidden_other = spread_hidden(hidden_kv)
    dq, own, one, two = attention(bias, queries[:, 0], grad_out[:, 0], kv0, kv1, kv2)

    one = shift(one, "core", 1)
    is_first = core == 0
    back = jnp.where(is_first, two, (two.astype(jnp.float32) + one.astype(jnp.float32)).astype(jnp.bfloat16))
    back = ctx_shift(back, -2)
    kv_grad = (own + back.astype(jnp.float32) + jnp.where(is_first, one.astype(jnp.float32), 0.0)).astype(jnp.bfloat16)
    heads = kv_grad.reshape(TOK, KV_HEADS, 2, HEAD_DIM)
    kv_out = heads.transpose(0, 2, 1, 3).reshape(TOK, 2 * KV_HEADS * HEAD_DIM)

    lo, hi = kv_grad[:, :512], kv_grad[:, 512:]
    mine = jnp.where(is_first, lo, hi)
    theirs = shift(jnp.where(is_first, hi, lo), "core", 1)
    block = jnp.concatenate([mine, theirs], axis=0)
    at = lax.axis_index(GATHER)
    gathered = [block] + [shift(block, GATHER, by) for by in (1, 2, 3)]

    acc = 0.0
    own_all = jnp.stack(hidden_own)
    other_all = jnp.stack(hidden_other)
    for by in range(4):
        seq = (at - by) % 4
        states = jnp.concatenate([pick(own_all, seq, 1), pick(other_all, seq, 1)], axis=1)
        acc = acc + lax.dot_general(states, gathered[by], (((1,), (0,)), ((), ())), preferred_element_type=jnp.float32)
    partial = acc.astype(jnp.bfloat16).reshape(4, 4, 80, 512)
    got = [pick(partial, x, 1)] + [shift(pick(partial, (x + by) % 4, 1), "x", by) for by in (1, 2, 3)]
    partial = total(got).astype(jnp.bfloat16)
    got = [partial[0]] + [shift(partial[by], SPREAD, -by) for by in (1, 2, 3)]
    partial = total(got).astype(jnp.bfloat16).reshape(2, 2, 20, 512)
    here, there = pick(partial, zh, 0), pick(partial, 1 - zh, 0)
    mine_here, mine_there = pick(here, core, 0), pick(there, core, 0)
    next_here, next_there = pick(here, 1 - core, 0), pick(there, 1 - core, 0)
    corner = lax.ppermute(next_there, ("zh", "core"), [(0, 3), (1, 2), (2, 1), (3, 0)])
    my_cols = total([mine_here, shift(mine_there, "zh", 1)])
    other_cols = total([shift(next_here, "core", 1), corner])
    cols = jnp.concatenate([jnp.where(is_first, my_cols, other_cols), jnp.where(is_first, other_cols, my_cols)], axis=1)
    weight = cols.reshape(20, KV_HEADS, 2, HEAD_DIM).transpose(0, 2, 1, 3).reshape(20, 2 * KV_HEADS * HEAD_DIM)
    return dq[:, None], kv_out[None], weight


def solution(mesh):
    fine = Mesh(mesh.devices.reshape(4, 4, 4, 2, 2), AXES)
    dp, ctx = ("zl", "y"), ("x", "zh", "core")
    placed = (
        P(None, dp, ctx, None),
        P(dp, ctx, None),
        P(None, dp, ctx, None),
        P(None, ctx, dp),
        P(dp, None),
    )
    return jax.shard_map(
        on_device,
        mesh=fine,
        in_specs=placed,
        out_specs=(P(None, dp, ctx, None), P(dp, ctx, None), P(dp + ctx, None)),
        check_vma=False,
    )
```

```python
import functools
import math

import jax
import jax.numpy as jnp
from jax import lax
from jax.experimental import pallas as pl
from jax.experimental.pallas import tpu as pltpu
from jax.sharding import Mesh, PartitionSpec as P

KV_HEADS = 4
GROUP = 5
HEAD_DIM = 128
LAYERS = 2
TOK = 128
CHUNKS = 2
PAIR = 2 * HEAD_DIM
FACTOR = 1.0 / math.sqrt(HEAD_DIM)
AXES = ("zl", "y", "x", "zh", "core")
SIZES = {"zl": 4, "y": 4, "x": 4, "zh": 2, "core": 2}


def shift(value, axis, by):
    size = SIZES[axis]
    return lax.ppermute(value, axis, [(i, (i + by) % size) for i in range(size)])


def ctx_shift(value, by):
    pairs = [(i, i + by) for i in range(16) if 0 <= i + by < 16]
    return lax.ppermute(value, ("x", "zh", "core"), pairs)


def z_shift(value, by):
    pairs = []
    for z in range(8):
        to = (z + by) % 8
        pairs.append(((z % 4) * 2 + z // 4, (to % 4) * 2 + to // 4))
    return lax.ppermute(value, ("zl", "zh"), pairs)


def attention_kernel(core_ref, bias_ref, q_ref, do_ref, k0_ref, k1_ref, k2_ref, v0_ref, v1_ref, v2_ref, *rest):
    dq_ref, theirs_ref, mine_ref = rest[-3:]
    keys = jnp.concatenate([k0_ref[...], k1_ref[...], k2_ref[...]], axis=0)
    values = jnp.concatenate([v0_ref[...], v1_ref[...], v2_ref[...]], axis=0)
    keys_t = keys.T
    bias = jnp.concatenate([bias_ref[...]] * LAYERS, axis=1)
    shape = (TOK, LAYERS * TOK)
    key_at = lax.broadcasted_iota(jnp.int32, shape, 0)
    query_at = lax.broadcasted_iota(jnp.int32, shape, 1) % TOK
    lower = key_at <= query_at
    lower_b = lower.astype(jnp.float32).astype(jnp.bfloat16)
    upper_b = 1 - lower_b
    nt = (((1,), (1,)), ((), ()))
    dk = jnp.zeros((3 * TOK, HEAD_DIM), jnp.float32)
    dv = jnp.zeros((3 * TOK, HEAD_DIM), jnp.float32)
    for g in range(GROUP):
        cols = slice(g * HEAD_DIM, (g + 1) * HEAD_DIM)
        q = jnp.concatenate([q_ref[0, :, cols], q_ref[1, :, cols]], axis=0)
        do = jnp.concatenate([do_ref[0, :, cols], do_ref[1, :, cols]], axis=0)
        s = lax.dot_general(keys, q, nt, preferred_element_type=jnp.float32)
        dp = lax.dot_general(values, do, nt, preferred_element_type=jnp.float32)
        s = jnp.concatenate([jnp.where(lower, s[:TOK], s[2 * TOK :]), s[TOK : 2 * TOK]], axis=0)
        dp = jnp.concatenate([jnp.where(lower, dp[:TOK], dp[2 * TOK :]), dp[TOK : 2 * TOK]], axis=0)
        s = s * (FACTOR * math.log2(math.e)) + bias
        e = jnp.exp2(s - jnp.max(s, axis=0, keepdims=True))
        p = e * (1.0 / jnp.sum(e, axis=0, keepdims=True))
        delta = jnp.sum(p * dp, axis=0, keepdims=True)
        ds = (p * (dp - delta)).astype(jnp.bfloat16)
        p = p.astype(jnp.bfloat16)
        p = jnp.concatenate([p[:TOK] * lower_b, p[TOK:], p[:TOK] * upper_b], axis=0)
        ds = jnp.concatenate([ds[:TOK] * lower_b, ds[TOK:], ds[:TOK] * upper_b], axis=0)
        dv += jnp.dot(p, do, preferred_element_type=jnp.float32)
        dk += jnp.dot(ds, q, preferred_element_type=jnp.float32)
        dq = jnp.dot(keys_t, ds, preferred_element_type=jnp.float32) * FACTOR
        dq = dq.astype(jnp.bfloat16).T
        dq_ref[0, :, cols] = dq[:TOK]
        dq_ref[1, :, cols] = dq[TOK:]
    both = jnp.concatenate([dk * FACTOR, dv], axis=1)

    @pl.when(pl.program_id(0) == 0)
    def _():
        theirs_ref[...] = both.astype(jnp.bfloat16)

    @pl.when(pl.program_id(0) == 1)
    def _():
        mine_ref[...] = both


def attention(chunk, core, bias, queries, grad_out, kv0, kv1, kv2, dq):
    wide = GROUP * HEAD_DIM

    def head(i, core_ref):
        return (1 - core_ref[0] + i) % 2

    rows = pl.BlockSpec((LAYERS, TOK, wide), lambda i, c: (0, 0, 2 * chunk + head(i, c)))
    key_cols = pl.BlockSpec((TOK, HEAD_DIM), lambda i, c: (0, head(i, c)))
    value_cols = pl.BlockSpec((TOK, HEAD_DIM), lambda i, c: (0, 2 + head(i, c)))
    whole = pl.BlockSpec((3 * TOK, PAIR), lambda i, c: (0, 0))
    operands = [bias, queries, grad_out, kv0, kv1, kv2, kv0, kv1, kv2]
    in_specs = [pl.BlockSpec((2 * TOK, TOK), lambda i, c: (0, 0)), rows, rows] + [key_cols] * 3 + [value_cols] * 3
    aliases = {}
    if dq is not None:
        operands.append(dq)
        in_specs.append(pl.BlockSpec(memory_space=pl.ANY))
        aliases = {len(operands): 0}
    return pl.pallas_call(
        attention_kernel,
        grid_spec=pltpu.PrefetchScalarGridSpec(
            num_scalar_prefetch=1,
            grid=(2,),
            in_specs=in_specs,
            out_specs=[rows, whole, whole],
        ),
        out_shape=[
            jax.ShapeDtypeStruct(queries.shape, jnp.bfloat16),
            jax.ShapeDtypeStruct((3 * TOK, PAIR), jnp.bfloat16),
            jax.ShapeDtypeStruct((3 * TOK, PAIR), jnp.float32),
        ],
        input_output_aliases=aliases,
        compiler_params=pltpu.CompilerParams(vmem_limit_bytes=32 * 1024 * 1024),
        cost_estimate=pl.CostEstimate(flops=3_000_000_000, bytes_accessed=5_000_000, transcendentals=700_000),
        name="attention",
    )(core[None], *operands)


def mask_bias(position, lengths):
    ends = jnp.cumsum(lengths)
    own = jnp.arange(TOK, dtype=jnp.int32)

    def doc(pos):
        return jnp.sum((pos[:, None] >= ends[None, :]).astype(jnp.int32), axis=1)

    query_doc = doc(position + own)
    zero, one, two = ((position - back * TOK + own) for back in (0, 1, 2))
    lower = own[:, None] <= own[None, :]
    seen = [(pos >= 0)[:, None] & (doc(pos)[:, None] == query_doc[None, :]) for pos in (zero, one, two)]
    seen = jnp.concatenate([jnp.where(lower, seen[0], seen[2]), seen[1]], axis=0)
    return jnp.where(seen, 0.0, -jnp.inf).astype(jnp.float32)


def pick(value, index, axis):
    return lax.dynamic_index_in_dim(value, index, axis, keepdims=False)


def total(parts):
    acc = parts[0].astype(jnp.float32)
    for part in parts[1:]:
        acc = acc + part.astype(jnp.float32)
    return acc


def on_device(queries, keys_values, grad_out, hidden_kv, doc_lengths):
    core, zh, x, y, zl = (lax.axis_index(name) for name in ("core", "zh", "x", "y", "zl"))
    first = core == 0
    position = ((x * 2 + zh) * 2 + core) * TOK
    kv = keys_values[0]
    half = KV_HEADS * HEAD_DIM
    windows = []
    for chunk in range(CHUNKS):
        at = chunk * PAIR
        kv0 = jnp.concatenate([kv[:, at : at + PAIR], kv[:, half + at : half + at + PAIR]], axis=1)
        kv2 = ctx_shift(kv0, 2)
        kv1 = shift(jnp.where(first, kv0, kv2), "core", 1)
        windows.append((kv0, kv1, kv2))
    bias = mask_bias(position, doc_lengths[0])

    hidden, _ = lax.optimization_barrier((hidden_kv, windows[-1][2]))
    hidden = hidden.reshape(4, 4, TOK, 320)
    states = [pick(hidden, zl, 0)] + [shift(pick(hidden, (zl + by) % 4, 0), "zl", by) for by in (1, 2, 3)]
    other_states = [shift(part, "core", 1) for part in states]

    dq = None
    halves = []
    for chunk in range(CHUNKS):
        dq, theirs, mine = attention(chunk, core, bias, queries[:, 0], grad_out[:, 0], *windows[chunk], dq)
        halves.append((mine, shift(theirs, "core", 1).astype(jnp.float32)))

    blocks = []
    for mine, got in halves:
        (m_own, m_one, m_two), (g_own, g_one, g_two) = mine.reshape(3, TOK, PAIR), got.reshape(3, TOK, PAIR)
        back = jnp.concatenate([m_two + jnp.where(first, 0.0, g_one), g_two + jnp.where(first, m_one, 0.0)], axis=0)
        back = ctx_shift(back.astype(jnp.bfloat16), -2).astype(jnp.float32)
        here = jnp.concatenate([m_own + jnp.where(first, g_one, 0.0), g_own + jnp.where(first, 0.0, m_one)], axis=0)
        blocks.append((here + back).astype(jnp.bfloat16))

    reduced = []
    for block in blocks:
        gathered = [block] + [shift(block, "y", by) for by in (1, 2, 3)]
        acc = 0.0
        for by in range(4):
            seq = (y - by) % 4
            rows = jnp.stack([jnp.concatenate([pick(a, seq, 0), pick(b, seq, 0)], axis=0) for a, b in zip(states, other_states)])
            acc = acc + lax.dot_general(rows, gathered[by], (((1,), (0,)), ((), ())), preferred_element_type=jnp.float32)
        partial = acc.astype(jnp.bfloat16).reshape(4, 4, 80, PAIR)
        got = [pick(partial, x, 1)] + [shift(pick(partial, (x + by) % 4, 1), "x", by) for by in (1, 2, 3)]
        reduced.append(total(got).astype(jnp.bfloat16))

    partial = jnp.concatenate(reduced, axis=2).reshape(4, 2, 40, 2 * PAIR)
    got = []
    for by in range(8):
        piece = pick(partial[-by % 4], (zh + (zl + by) // 4) % 2, 0)
        got.append(z_shift(piece, by) if by else piece)
    rows = total(got).reshape(2, 20, 2 * PAIR)
    ours = pick(rows, core, 0)
    others = shift(pick(rows, 1 - core, 0), "core", 1)

    def assemble(own, other):
        count = own.shape[0]
        own = own.reshape(count, CHUNKS, 1, 2, HEAD_DIM)
        other = other.reshape(count, CHUNKS, 1, 2, HEAD_DIM)
        heads = jnp.concatenate([jnp.where(first, own, other), jnp.where(first, other, own)], axis=2)
        return heads.transpose(0, 3, 1, 2, 4).reshape(count, 2 * KV_HEADS * HEAD_DIM)

    weight = assemble(ours, others)
    block = jnp.concatenate(blocks, axis=1)
    kv_out = assemble(block[:TOK], shift(block[TOK:], "core", 1))
    return dq[:, None], kv_out[None], weight


def solution(mesh):
    fine = Mesh(mesh.devices.reshape(4, 4, 4, 2, 2), AXES)
    dp, ctx = ("zl", "y"), ("x", "zh", "core")
    placed = (
        P(None, dp, ctx, None),
        P(dp, ctx, None),
        P(None, dp, ctx, None),
        P(None, ctx, dp),
        P(dp, None),
    )
    return jax.shard_map(
        on_device,
        mesh=fine,
        in_specs=placed,
        out_specs=(P(None, dp, ctx, None), P(dp, ctx, None), P(dp + ctx, None)),
        check_vma=False,
    )
```

```python
import functools
import math

import jax
import jax.numpy as jnp
from jax import lax
from jax.experimental import pallas as pl
from jax.experimental.pallas import tpu as pltpu
from jax.sharding import Mesh, PartitionSpec as P

KV_HEADS = 4
GROUP = 5
HEAD_DIM = 128
LAYERS = 2
TOK = 128
WIDE = 320
VMEM = 60 * 1024 * 1024
PAIR = 2 * HEAD_DIM
FACTOR = 1.0 / math.sqrt(HEAD_DIM)
AXES = ("zl", "y", "x", "zh", "core")
SIZES = {"zl": 4, "y": 4, "x": 4, "zh": 2, "core": 2}


def shift(value, axis, by):
    size = SIZES[axis]
    return lax.ppermute(value, axis, [(i, (i + by) % size) for i in range(size)])


def ctx_shift(value, by):
    pairs = [(i, i + by) for i in range(16) if 0 <= i + by < 16]
    return lax.ppermute(value, ("x", "zh", "core"), pairs)


def softmax_grad(s, dp, bias, lower, lower_b, upper_b):
    scale = FACTOR * math.log2(math.e)
    s0 = jnp.where(lower, s[:TOK], s[2 * TOK :]) * scale + bias[:TOK]
    s1 = s[TOK : 2 * TOK] * scale + bias[TOK:]
    top = jnp.max(jnp.maximum(s0, s1), axis=0, keepdims=True)
    e0, e1 = jnp.exp2(s0 - top), jnp.exp2(s1 - top)
    inv = 1.0 / jnp.sum(e0 + e1, axis=0, keepdims=True)
    p0, p1 = e0 * inv, e1 * inv
    d0 = p0 * jnp.where(lower, dp[:TOK], dp[2 * TOK :])
    d1 = p1 * dp[TOK : 2 * TOK]
    delta = jnp.sum(d0 + d1, axis=0, keepdims=True)
    d0, d1 = (d0 - p0 * delta).astype(jnp.bfloat16), (d1 - p1 * delta).astype(jnp.bfloat16)
    p0, p1 = p0.astype(jnp.bfloat16), p1.astype(jnp.bfloat16)
    p = jnp.concatenate([p0 * lower_b, p1, p0 * upper_b], axis=0)
    ds = jnp.concatenate([d0 * lower_b, d1, d0 * upper_b], axis=0)
    return p, ds


def attention_kernel(core_ref, bias_ref, q_ref, do_ref, k0_ref, k1_ref, k2_ref, v0_ref, v1_ref, v2_ref, dq_ref, theirs_ref, mine_ref):
    keys = jnp.concatenate([k0_ref[...], k1_ref[...], k2_ref[...]], axis=0)
    values = jnp.concatenate([v0_ref[...], v1_ref[...], v2_ref[...]], axis=0)
    keys_t = keys.T
    bias = bias_ref[...]
    key_at = lax.broadcasted_iota(jnp.int32, (TOK, TOK), 0)
    query_at = lax.broadcasted_iota(jnp.int32, (TOK, TOK), 1)
    lower = key_at <= query_at
    lower_b = lower.astype(jnp.float32).astype(jnp.bfloat16)
    upper_b = 1 - lower_b
    nt = (((1,), (1,)), ((), ()))

    def load(g):
        cols = slice(g * HEAD_DIM, (g + 1) * HEAD_DIM)
        q = jnp.concatenate([q_ref[0, :, cols], q_ref[1, :, cols]], axis=0)
        do = jnp.concatenate([do_ref[0, :, cols], do_ref[1, :, cols]], axis=0)
        s = lax.dot_general(keys, q, nt, preferred_element_type=jnp.float32)
        dp = lax.dot_general(values, do, nt, preferred_element_type=jnp.float32)
        return q, do, s, dp

    def store(g, q, do, p, ds, dk, dv):
        cols = slice(g * HEAD_DIM, (g + 1) * HEAD_DIM)
        dv += jnp.dot(p, do, preferred_element_type=jnp.float32)
        dk += jnp.dot(ds, q, preferred_element_type=jnp.float32)
        dq = jnp.dot(keys_t, ds, preferred_element_type=jnp.float32) * FACTOR
        dq = dq.astype(jnp.bfloat16).T
        dq_ref[0, :, cols] = dq[:TOK]
        dq_ref[1, :, cols] = dq[TOK:]
        return dk, dv

    dk = jnp.zeros((3 * TOK, HEAD_DIM), jnp.float32)
    dv = jnp.zeros((3 * TOK, HEAD_DIM), jnp.float32)
    following, done = load(0), None
    for g in range(GROUP):
        q, do, s, dp = following
        if g + 1 < GROUP:
            following = load(g + 1)
        if done is not None:
            dk, dv = store(*done, dk, dv)
        tiles = [slice(layer * TOK, (layer + 1) * TOK) for layer in range(LAYERS)]
        parts = [softmax_grad(s[:, t], dp[:, t], bias, lower, lower_b, upper_b) for t in tiles]
        p = jnp.concatenate([part[0] for part in parts], axis=1)
        ds = jnp.concatenate([part[1] for part in parts], axis=1)
        done = (g, q, do, p, ds)
    dk, dv = store(*done, dk, dv)
    both = jnp.concatenate([dk * FACTOR, dv], axis=1)

    @pl.when(pl.program_id(0) < 2)
    def _():
        theirs_ref[...] = both.astype(jnp.bfloat16)

    @pl.when(pl.program_id(0) >= 2)
    def _():
        mine_ref[...] = both


def attention(core, bias, queries, grad_out, kv0, kv1, kv2):
    wide = GROUP * HEAD_DIM

    def head(i, core_ref):
        return (2 - 2 * core_ref[0] + i) % KV_HEADS

    rows = pl.BlockSpec((LAYERS, TOK, wide), lambda i, c: (0, 0, head(i, c)))
    key_cols = pl.BlockSpec((TOK, HEAD_DIM), lambda i, c: (0, head(i, c)))
    value_cols = pl.BlockSpec((TOK, HEAD_DIM), lambda i, c: (0, KV_HEADS + head(i, c)))
    theirs = pl.BlockSpec((3 * TOK, PAIR), lambda i, c: (0, jnp.minimum(i, 1)))
    mine = pl.BlockSpec((3 * TOK, PAIR), lambda i, c: (0, jnp.maximum(i - 2, 0)))
    return pl.pallas_call(
        attention_kernel,
        grid_spec=pltpu.PrefetchScalarGridSpec(
            num_scalar_prefetch=1,
            grid=(KV_HEADS,),
            in_specs=[pl.BlockSpec((2 * TOK, TOK), lambda i, c: (0, 0)), rows, rows] + [key_cols] * 3 + [value_cols] * 3,
            out_specs=[rows, theirs, mine],
        ),
        out_shape=[
            jax.ShapeDtypeStruct(queries.shape, jnp.bfloat16),
            jax.ShapeDtypeStruct((3 * TOK, 2 * PAIR), jnp.bfloat16),
            jax.ShapeDtypeStruct((3 * TOK, 2 * PAIR), jnp.float32),
        ],
        compiler_params=pltpu.CompilerParams(vmem_limit_bytes=VMEM),
        cost_estimate=pl.CostEstimate(flops=6_000_000_000, bytes_accessed=9_000_000, transcendentals=1_400_000),
        name="attention",
    )(core[None], bias, queries, grad_out, kv0, kv1, kv2, kv0, kv1, kv2)


def product_kernel(at_ref, own_ref, other_ref, *refs):
    block_refs, out_refs, acc_ref = refs[:4], refs[4:8], refs[8]
    zl, x = at_ref[0], at_ref[1]
    left = []
    for by in range(4):
        seq = (zl - by + 4) % 4
        left += [own_ref[0, seq], other_ref[0, seq]]
    left = jnp.concatenate(left, axis=1)
    right = jnp.concatenate([ref[...] for ref in block_refs], axis=0)
    acc_ref[...] = jnp.dot(left, right, preferred_element_type=jnp.float32)
    for by in range(4):
        start = pl.multiple_of((x + by) % 4 * 80, 16)
        out_refs[by][0] = acc_ref[pl.ds(start, 80)].astype(jnp.bfloat16)


def products(at, own, other, blocks):
    states = pl.BlockSpec((1, 4, WIDE, TOK), lambda i, at: ((at[2] - i + 4) % 4, 0, 0, 0))
    return pl.pallas_call(
        product_kernel,
        grid_spec=pltpu.PrefetchScalarGridSpec(
            num_scalar_prefetch=1,
            grid=(4,),
            in_specs=[states, states] + [pl.BlockSpec((2 * TOK, PAIR), lambda i, at: (0, 0))] * 4,
            out_specs=[pl.BlockSpec((1, 80, PAIR), lambda i, at: (i, 0, 0))] * 4,
            scratch_shapes=[pltpu.VMEM((WIDE, PAIR), jnp.float32)],
        ),
        out_shape=[jax.ShapeDtypeStruct((4, 80, PAIR), jnp.bfloat16)] * 4,
        compiler_params=pltpu.CompilerParams(vmem_limit_bytes=16 * 1024 * 1024),
        cost_estimate=pl.CostEstimate(flops=1_400_000_000, bytes_accessed=5_000_000, transcendentals=0),
        name="products",
    )(at, own, other, *blocks)


def mask_bias(position, ends):
    own = jnp.arange(TOK, dtype=jnp.int32)

    def doc(pos):
        return jnp.sum((pos[:, None] >= ends[None, :]).astype(jnp.int32), axis=1)

    query_doc = doc(position + own)
    zero, one, two = ((position - back * TOK + own) for back in (0, 1, 2))
    lower = own[:, None] <= own[None, :]
    seen = [(pos >= 0)[:, None] & (doc(pos)[:, None] == query_doc[None, :]) for pos in (zero, one, two)]
    seen = jnp.concatenate([jnp.where(lower, seen[0], seen[2]), seen[1]], axis=0)
    return jnp.where(seen, 0.0, -jnp.inf).astype(jnp.float32)


def pick(value, index, axis):
    return lax.dynamic_index_in_dim(value, index, axis, keepdims=False)


def total(parts):
    acc = parts[0].astype(jnp.float32)
    for part in parts[1:]:
        acc = acc + part.astype(jnp.float32)
    return acc


def on_device(queries, keys_values, grad_out, hidden_kv, doc_lengths):
    core, zh, x, y, zl = (lax.axis_index(name) for name in ("core", "zh", "x", "y", "zl"))
    first = core == 0
    position = ((x * 2 + zh) * 2 + core) * TOK
    kv = keys_values[0]
    half = KV_HEADS * HEAD_DIM
    kv2 = ctx_shift(kv, 2)
    kv1 = shift(jnp.where(first, kv, kv2), "core", 1)

    bias = mask_bias(position, jnp.cumsum(doc_lengths[0]))
    hidden = hidden_kv.transpose(0, 2, 1).reshape(4, 4, WIDE, TOK)
    states = [pick(hidden, y, 1)] + [shift(pick(hidden, (y + by) % 4, 1), "y", by) for by in (1, 2, 3)]

    dq, theirs, mine = attention(core, bias, queries[:, 0], grad_out[:, 0], kv, kv1, kv2)
    states, theirs = lax.optimization_barrier((states, theirs))
    theirs = shift(theirs, "core", 1)
    halves = []
    for part in range(2):
        cols = slice(part * PAIR, (part + 1) * PAIR)
        (m_own, m_one, m_two), (g_own, g_one, g_two) = mine[:, cols].reshape(3, TOK, PAIR), theirs[:, cols].reshape(3, TOK, PAIR)
        g_own, g_one, g_two = (term.astype(jnp.float32) for term in (g_own, g_one, g_two))
        back = jnp.concatenate([m_two + jnp.where(first, 0.0, g_one), g_two + jnp.where(first, m_one, 0.0)], axis=0)
        here = jnp.concatenate([m_own + jnp.where(first, g_one, 0.0), g_own + jnp.where(first, 0.0, m_one)], axis=0)
        back = back.astype(jnp.bfloat16)
        halves.append((here, ctx_shift(back, -2)))

    states, _ = lax.optimization_barrier((states, back))
    states = jnp.stack(states)
    other_states = shift(states, "core", 1)

    blocks, reduced = [], []
    for here, came in halves:
        block = (here + came.astype(jnp.float32)).astype(jnp.bfloat16)
        blocks.append(block)
        gathered = [block] + [shift(block, "zl", by) for by in (1, 2, 3)]
        pieces = products(jnp.stack([zl, x, y]).astype(jnp.int32), states, other_states, gathered)
        got = [pieces[0]] + [shift(pieces[by], "x", by) for by in (1, 2, 3)]
        reduced.append(total(got).astype(jnp.bfloat16))
    block = jnp.concatenate(blocks, axis=1)
    partial = jnp.concatenate(reduced, axis=2)

    got = lax.all_to_all(partial.reshape(8, 40, 2 * PAIR), ("y", "zh"), 0, 0)
    rows = jnp.sum(got.astype(jnp.float32), axis=0).reshape(2, 20, 2 * PAIR)
    ours = pick(rows, core, 0)
    others = shift(pick(rows, 1 - core, 0), "core", 1)

    def assemble(own, other):
        count = own.shape[0]
        cols = jnp.concatenate([jnp.where(first, own, other), jnp.where(first, other, own)], axis=1)
        return cols.reshape(count, KV_HEADS, 2, HEAD_DIM).transpose(0, 2, 1, 3).reshape(count, KV_HEADS * PAIR)

    weight = assemble(ours, others)
    kv_out = assemble(block[:TOK], shift(block[TOK:], "core", 1))
    return dq[:, None], kv_out[None], weight


def solution(mesh):
    fine = Mesh(mesh.devices.reshape(4, 4, 4, 2, 2), AXES)
    dp, ctx = ("zl", "y"), ("x", "zh", "core")
    placed = (
        P(None, dp, ctx, None),
        P(dp, ctx, None),
        P(None, dp, ctx, None),
        P(None, ctx, dp),
        P(dp, None),
    )
    return jax.shard_map(
        on_device,
        mesh=fine,
        in_specs=placed,
        out_specs=(P(None, dp, ctx, None), P(dp, ctx, None), P(dp + ctx, None)),
        check_vma=False,
    )
```

```python
import functools
import math

import jax
import jax.numpy as jnp
from jax import lax
from jax.experimental import pallas as pl
from jax.experimental.pallas import tpu as pltpu
from jax.sharding import Mesh, PartitionSpec as P

KV_HEADS = 4
GROUP = 5
HEAD_DIM = 128
LAYERS = 2
TOK = 128
WIDE = 320
VMEM = 60 * 1024 * 1024
PAIR = 2 * HEAD_DIM
FACTOR = 1.0 / math.sqrt(HEAD_DIM)
AXES = ("zl", "y", "x", "zh", "core")
SIZES = {"zl": 4, "y": 4, "x": 4, "zh": 2, "core": 2}


def shift(value, axis, by):
    size = SIZES[axis]
    return lax.ppermute(value, axis, [(i, (i + by) % size) for i in range(size)])


def ctx_shift(value, by):
    pairs = [(i, i + by) for i in range(16) if 0 <= i + by < 16]
    return lax.ppermute(value, ("x", "zh", "core"), pairs)


def softmax_grad(s, dp, bias, lower, lower_b, upper_b):
    scale = FACTOR * math.log2(math.e)
    s0 = jnp.where(lower, s[:TOK], s[2 * TOK :]) * scale + bias[:TOK]
    s1 = s[TOK : 2 * TOK] * scale + bias[TOK:]
    top = jnp.max(jnp.maximum(s0, s1), axis=0, keepdims=True)
    e0, e1 = jnp.exp2(s0 - top), jnp.exp2(s1 - top)
    inv = 1.0 / jnp.sum(e0 + e1, axis=0, keepdims=True)
    p0, p1 = e0 * inv, e1 * inv
    d0 = p0 * jnp.where(lower, dp[:TOK], dp[2 * TOK :])
    d1 = p1 * dp[TOK : 2 * TOK]
    delta = jnp.sum(d0 + d1, axis=0, keepdims=True)
    d0, d1 = (d0 - p0 * delta).astype(jnp.bfloat16), (d1 - p1 * delta).astype(jnp.bfloat16)
    p0, p1 = p0.astype(jnp.bfloat16), p1.astype(jnp.bfloat16)
    p = jnp.concatenate([p0 * lower_b, p1, p0 * upper_b], axis=0)
    ds = jnp.concatenate([d0 * lower_b, d1, d0 * upper_b], axis=0)
    return p, ds


def attention_kernel(core_ref, bias_ref, q_ref, do_ref, kv0_ref, kv1_ref, kv2_ref, dq_ref, theirs_ref, mine_ref):
    head = (2 - 2 * core_ref[0] + pl.program_id(0)) % KV_HEADS
    key_cols = pl.ds(pl.multiple_of(head * HEAD_DIM, HEAD_DIM), HEAD_DIM)
    value_cols = pl.ds(pl.multiple_of((KV_HEADS + head) * HEAD_DIM, HEAD_DIM), HEAD_DIM)
    keys = jnp.concatenate([ref[:, key_cols] for ref in (kv0_ref, kv1_ref, kv2_ref)], axis=0)
    values = jnp.concatenate([ref[:, value_cols] for ref in (kv0_ref, kv1_ref, kv2_ref)], axis=0)
    keys_t = keys.T
    bias = bias_ref[...]
    key_at = lax.broadcasted_iota(jnp.int32, (TOK, TOK), 0)
    query_at = lax.broadcasted_iota(jnp.int32, (TOK, TOK), 1)
    lower = key_at <= query_at
    lower_b = lower.astype(jnp.float32).astype(jnp.bfloat16)
    upper_b = 1 - lower_b
    nt = (((1,), (1,)), ((), ()))

    def load(g):
        cols = slice(g * HEAD_DIM, (g + 1) * HEAD_DIM)
        q = jnp.concatenate([q_ref[0, :, cols], q_ref[1, :, cols]], axis=0)
        do = jnp.concatenate([do_ref[0, :, cols], do_ref[1, :, cols]], axis=0)
        s = lax.dot_general(keys, q, nt, preferred_element_type=jnp.float32)
        dp = lax.dot_general(values, do, nt, preferred_element_type=jnp.float32)
        return q, do, s, dp

    def store(g, q, do, p, ds, dk, dv):
        cols = slice(g * HEAD_DIM, (g + 1) * HEAD_DIM)
        dv += jnp.dot(p, do, preferred_element_type=jnp.float32)
        dk += jnp.dot(ds, q, preferred_element_type=jnp.float32)
        dq = jnp.dot(keys_t, ds, preferred_element_type=jnp.float32) * FACTOR
        dq = dq.astype(jnp.bfloat16).T
        dq_ref[0, :, cols] = dq[:TOK]
        dq_ref[1, :, cols] = dq[TOK:]
        return dk, dv

    dk = jnp.zeros((3 * TOK, HEAD_DIM), jnp.float32)
    dv = jnp.zeros((3 * TOK, HEAD_DIM), jnp.float32)
    following, done = load(0), None
    for g in range(GROUP):
        q, do, s, dp = following
        if g + 1 < GROUP:
            following = load(g + 1)
        if done is not None:
            dk, dv = store(*done, dk, dv)
        tiles = [slice(layer * TOK, (layer + 1) * TOK) for layer in range(LAYERS)]
        parts = [softmax_grad(s[:, t], dp[:, t], bias, lower, lower_b, upper_b) for t in tiles]
        p = jnp.concatenate([part[0] for part in parts], axis=1)
        ds = jnp.concatenate([part[1] for part in parts], axis=1)
        done = (g, q, do, p, ds)
    dk, dv = store(*done, dk, dv)
    both = jnp.concatenate([dk * FACTOR, dv], axis=1)

    @pl.when(pl.program_id(0) < 2)
    def _():
        theirs_ref[...] = both.astype(jnp.bfloat16)

    @pl.when(pl.program_id(0) >= 2)
    def _():
        mine_ref[...] = both


def attention(core, bias, queries, grad_out, kv0, kv1, kv2):
    wide = GROUP * HEAD_DIM

    def head(i, core_ref):
        return (2 - 2 * core_ref[0] + i) % KV_HEADS

    rows = pl.BlockSpec((LAYERS, TOK, wide), lambda i, c: (0, 0, head(i, c)))
    held = pl.BlockSpec(memory_space=pltpu.VMEM)
    theirs = pl.BlockSpec((3 * TOK, PAIR), lambda i, c: (0, jnp.minimum(i, 1)))
    mine = pl.BlockSpec((3 * TOK, PAIR), lambda i, c: (0, jnp.maximum(i - 2, 0)))
    return pl.pallas_call(
        attention_kernel,
        grid_spec=pltpu.PrefetchScalarGridSpec(
            num_scalar_prefetch=1,
            grid=(KV_HEADS,),
            in_specs=[held, rows, rows, held, held, held],
            out_specs=[rows, theirs, mine],
        ),
        out_shape=[
            jax.ShapeDtypeStruct(queries.shape, jnp.bfloat16),
            jax.ShapeDtypeStruct((3 * TOK, 2 * PAIR), jnp.bfloat16),
            jax.ShapeDtypeStruct((3 * TOK, 2 * PAIR), jnp.float32),
        ],
        compiler_params=pltpu.CompilerParams(vmem_limit_bytes=VMEM),
        cost_estimate=pl.CostEstimate(flops=6_000_000_000, bytes_accessed=9_000_000, transcendentals=1_400_000),
        name="attention",
    )(core[None], bias, queries, grad_out, kv0, kv1, kv2)


def product_kernel(at_ref, own_ref, other_ref, *refs):
    block_refs, out_refs, acc_ref = refs[:4], refs[4:8], refs[8]
    zl, x = at_ref[0], at_ref[1]
    left = []
    for by in range(4):
        seq = (zl - by + 4) % 4
        left += [own_ref[0, seq], other_ref[0, seq]]
    left = jnp.concatenate(left, axis=1)
    right = jnp.concatenate([ref[...] for ref in block_refs], axis=0)
    acc_ref[...] = jnp.dot(left, right, preferred_element_type=jnp.float32)
    for by in range(4):
        start = pl.multiple_of((x + by) % 4 * 80, 16)
        out_refs[by][0] = acc_ref[pl.ds(start, 80)].astype(jnp.bfloat16)


def products(at, own, other, blocks):
    states = pl.BlockSpec((1, 4, WIDE, TOK), lambda i, at: ((at[2] - i + 4) % 4, 0, 0, 0))
    return pl.pallas_call(
        product_kernel,
        grid_spec=pltpu.PrefetchScalarGridSpec(
            num_scalar_prefetch=1,
            grid=(4,),
            in_specs=[states, states] + [pl.BlockSpec((2 * TOK, PAIR), lambda i, at: (0, 0))] * 4,
            out_specs=[pl.BlockSpec((1, 80, PAIR), lambda i, at: (i, 0, 0))] * 4,
            scratch_shapes=[pltpu.VMEM((WIDE, PAIR), jnp.float32)],
        ),
        out_shape=[jax.ShapeDtypeStruct((4, 80, PAIR), jnp.bfloat16)] * 4,
        compiler_params=pltpu.CompilerParams(vmem_limit_bytes=16 * 1024 * 1024),
        cost_estimate=pl.CostEstimate(flops=1_400_000_000, bytes_accessed=5_000_000, transcendentals=0),
        name="products",
    )(at, own, other, *blocks)


def mask_bias(position, ends):
    own = jnp.arange(TOK, dtype=jnp.int32)

    def doc(pos):
        return jnp.sum((pos[:, None] >= ends[None, :]).astype(jnp.int32), axis=1)

    query_doc = doc(position + own)
    zero, one, two = ((position - back * TOK + own) for back in (0, 1, 2))
    lower = own[:, None] <= own[None, :]
    seen = [(pos >= 0)[:, None] & (doc(pos)[:, None] == query_doc[None, :]) for pos in (zero, one, two)]
    seen = jnp.concatenate([jnp.where(lower, seen[0], seen[2]), seen[1]], axis=0)
    return jnp.where(seen, 0.0, -jnp.inf).astype(jnp.float32)


def pick(value, index, axis):
    return lax.dynamic_index_in_dim(value, index, axis, keepdims=False)


def total(parts):
    acc = parts[0].astype(jnp.float32)
    for part in parts[1:]:
        acc = acc + part.astype(jnp.float32)
    return acc


def on_device(queries, keys_values, grad_out, hidden_kv, doc_lengths):
    core, zh, x, y, zl = (lax.axis_index(name) for name in ("core", "zh", "x", "y", "zl"))
    first = core == 0
    position = ((x * 2 + zh) * 2 + core) * TOK
    kv = keys_values[0]
    half = KV_HEADS * HEAD_DIM
    kv2 = ctx_shift(kv, 2)
    kv1 = shift(jnp.where(first, kv, kv2), "core", 1)

    bias = mask_bias(position, jnp.cumsum(doc_lengths[0]))
    hidden = hidden_kv.transpose(0, 2, 1).reshape(4, 4, WIDE, TOK)
    states = [pick(hidden, y, 1)] + [shift(pick(hidden, (y + by) % 4, 1), "y", by) for by in (1, 2, 3)]

    dq, theirs, mine = attention(core, bias, queries[:, 0], grad_out[:, 0], kv, kv1, kv2)
    states, theirs = lax.optimization_barrier((states, theirs))
    theirs = shift(theirs, "core", 1)
    def terms(cols):
        mine_terms = mine[:, cols].reshape(3, TOK, PAIR)
        got_terms = theirs[:, cols].reshape(3, TOK, PAIR).astype(jnp.float32)
        return mine_terms, got_terms

    cameback = []
    parts = [slice(0, PAIR), slice(PAIR, 2 * PAIR)]
    for cols in parts:
        (_, m_one, m_two), (_, g_one, g_two) = terms(cols)
        back = jnp.concatenate([m_two + jnp.where(first, 0.0, g_one), g_two + jnp.where(first, m_one, 0.0)], axis=0)
        back = back.astype(jnp.bfloat16)
        cameback.append(ctx_shift(back, -2))

    mine, theirs, _ = lax.optimization_barrier((mine, theirs, back))
    halves = []
    for cols, came in zip(parts, cameback):
        (m_own, m_one, _), (g_own, g_one, _) = terms(cols)
        here = jnp.concatenate([m_own + jnp.where(first, g_one, 0.0), g_own + jnp.where(first, 0.0, m_one)], axis=0)
        halves.append((here, came))
    states, _ = lax.optimization_barrier((states, here))
    states = jnp.stack(states)
    other_states = shift(states, "core", 1)

    blocks, reduced = [], []
    for here, came in halves:
        block = (here + came.astype(jnp.float32)).astype(jnp.bfloat16)
        blocks.append(block)
        gathered = [block] + [shift(block, "zl", by) for by in (1, 2, 3)]
        pieces = products(jnp.stack([zl, x, y]).astype(jnp.int32), states, other_states, gathered)
        got = [pieces[0]] + [shift(pieces[by], "x", by) for by in (1, 2, 3)]
        reduced.append(total(got).astype(jnp.bfloat16))
    block = jnp.concatenate(blocks, axis=1)
    partial = []
    for part in reduced:
        got = [pick(part, y, 0)] + [shift(pick(part, (y + by) % 4, 0), "y", by) for by in (1, 2, 3)]
        partial.append(total(got).astype(jnp.bfloat16))
    partial = jnp.concatenate(partial, axis=1).reshape(2, 40, 2 * PAIR)
    rows = total([pick(partial, zh, 0), shift(pick(partial, 1 - zh, 0), "zh", 1)]).reshape(2, 20, 2 * PAIR)
    ours = pick(rows, core, 0)
    others = shift(pick(rows, 1 - core, 0), "core", 1)
    def assemble(own, other):
        count = own.shape[0]
        cols = jnp.concatenate([jnp.where(first, own, other), jnp.where(first, other, own)], axis=1)
        return cols.reshape(count, KV_HEADS, 2, HEAD_DIM).transpose(0, 2, 1, 3).reshape(count, KV_HEADS * PAIR)

    low, high = jnp.where(first, ours, others), jnp.where(first, others, ours)
    heads = [part[:, i * HEAD_DIM : (i + 1) * HEAD_DIM] for part in (low, high) for i in range(4)]
    weight = jnp.concatenate(heads[0::2] + heads[1::2], axis=1)
    kv_out = assemble(block[:TOK], shift(block[TOK:], "core", 1))
    return dq[:, None], kv_out[None], weight


def solution(mesh):
    fine = Mesh(mesh.devices.reshape(4, 4, 4, 2, 2), AXES)
    dp, ctx = ("zl", "y"), ("x", "zh", "core")
    placed = (
        P(None, dp, ctx, None),
        P(dp, ctx, None),
        P(None, dp, ctx, None),
        P(None, ctx, dp),
        P(dp, None),
    )
    return jax.shard_map(
        on_device,
        mesh=fine,
        in_specs=placed,
        out_specs=(P(None, dp, ctx, None), P(dp, ctx, None), P(dp + ctx, None)),
        check_vma=False,
    )
```

```python
import functools
import math

import jax
import jax.numpy as jnp
from jax import lax
from jax.experimental import pallas as pl
from jax.experimental.pallas import tpu as pltpu
from jax.sharding import Mesh, PartitionSpec as P

KV_HEADS = 4
GROUP = 5
HEAD_DIM = 128
LAYERS = 2
TOK = 128
WIDE = 320
VMEM = 60 * 1024 * 1024
PAIR = 2 * HEAD_DIM
FACTOR = 1.0 / math.sqrt(HEAD_DIM)
AXES = ("zl", "y", "x", "zh", "core")
SIZES = {"zl": 4, "y": 4, "x": 4, "zh": 2, "core": 2}


def shift(value, axis, by):
    size = SIZES[axis]
    return lax.ppermute(value, axis, [(i, (i + by) % size) for i in range(size)])


def ctx_shift(value, by):
    pairs = [(i, i + by) for i in range(16) if 0 <= i + by < 16]
    return lax.ppermute(value, ("x", "zh", "core"), pairs)


def softmax_grad(s, dp, bias, lower, lower_b, upper_b):
    scale = FACTOR * math.log2(math.e)
    s0 = jnp.where(lower, s[:TOK], s[2 * TOK :]) * scale + bias[:TOK]
    s1 = s[TOK : 2 * TOK] * scale + bias[TOK:]
    top = jnp.max(jnp.maximum(s0, s1), axis=0, keepdims=True)
    e0, e1 = jnp.exp2(s0 - top), jnp.exp2(s1 - top)
    inv = 1.0 / jnp.sum(e0 + e1, axis=0, keepdims=True)
    p0, p1 = e0 * inv, e1 * inv
    d0 = p0 * jnp.where(lower, dp[:TOK], dp[2 * TOK :])
    d1 = p1 * dp[TOK : 2 * TOK]
    delta = jnp.sum(d0 + d1, axis=0, keepdims=True)
    d0, d1 = (d0 - p0 * delta).astype(jnp.bfloat16), (d1 - p1 * delta).astype(jnp.bfloat16)
    p0, p1 = p0.astype(jnp.bfloat16), p1.astype(jnp.bfloat16)
    p = jnp.concatenate([p0 * lower_b, p1, p0 * upper_b], axis=0)
    ds = jnp.concatenate([d0 * lower_b, d1, d0 * upper_b], axis=0)
    return p, ds


def attention_kernel(core_ref, bias_ref, q_ref, do_ref, kv0_ref, kv1_ref, kv2_ref, dq_ref, theirs_ref, mine_ref):
    head = (2 - 2 * core_ref[0] + pl.program_id(0)) % KV_HEADS
    key_cols = pl.ds(pl.multiple_of(head * HEAD_DIM, HEAD_DIM), HEAD_DIM)
    value_cols = pl.ds(pl.multiple_of((KV_HEADS + head) * HEAD_DIM, HEAD_DIM), HEAD_DIM)
    keys = jnp.concatenate([ref[:, key_cols] for ref in (kv0_ref, kv1_ref, kv2_ref)], axis=0)
    values = jnp.concatenate([ref[:, value_cols] for ref in (kv0_ref, kv1_ref, kv2_ref)], axis=0)
    keys_t = keys.T
    bias = bias_ref[...]
    key_at = lax.broadcasted_iota(jnp.int32, (TOK, TOK), 0)
    query_at = lax.broadcasted_iota(jnp.int32, (TOK, TOK), 1)
    lower = key_at <= query_at
    lower_b = lower.astype(jnp.float32).astype(jnp.bfloat16)
    upper_b = 1 - lower_b
    nt = (((1,), (1,)), ((), ()))

    def load(g):
        cols = slice(g * HEAD_DIM, (g + 1) * HEAD_DIM)
        q = jnp.concatenate([q_ref[0, :, cols], q_ref[1, :, cols]], axis=0)
        do = jnp.concatenate([do_ref[0, :, cols], do_ref[1, :, cols]], axis=0)
        s = lax.dot_general(keys, q, nt, preferred_element_type=jnp.float32)
        dp = lax.dot_general(values, do, nt, preferred_element_type=jnp.float32)
        return q, do, s, dp

    def store(g, q, do, p, ds, dk, dv):
        cols = slice(g * HEAD_DIM, (g + 1) * HEAD_DIM)
        dv += jnp.dot(p, do, preferred_element_type=jnp.float32)
        dk += jnp.dot(ds, q, preferred_element_type=jnp.float32)
        dq = jnp.dot(keys_t, ds, preferred_element_type=jnp.float32) * FACTOR
        dq = dq.astype(jnp.bfloat16).T
        dq_ref[0, :, cols] = dq[:TOK]
        dq_ref[1, :, cols] = dq[TOK:]
        return dk, dv

    dk = jnp.zeros((3 * TOK, HEAD_DIM), jnp.float32)
    dv = jnp.zeros((3 * TOK, HEAD_DIM), jnp.float32)
    following, done = load(0), None
    for g in range(GROUP):
        q, do, s, dp = following
        if g + 1 < GROUP:
            following = load(g + 1)
        if done is not None:
            dk, dv = store(*done, dk, dv)
        tiles = [slice(layer * TOK, (layer + 1) * TOK) for layer in range(LAYERS)]
        parts = [softmax_grad(s[:, t], dp[:, t], bias, lower, lower_b, upper_b) for t in tiles]
        p = jnp.concatenate([part[0] for part in parts], axis=1)
        ds = jnp.concatenate([part[1] for part in parts], axis=1)
        done = (g, q, do, p, ds)
    dk, dv = store(*done, dk, dv)
    both = jnp.concatenate([dk * FACTOR, dv], axis=1)

    @pl.when(pl.program_id(0) < 2)
    def _():
        theirs_ref[...] = both.astype(jnp.bfloat16)

    @pl.when(pl.program_id(0) >= 2)
    def _():
        mine_ref[...] = both


def attention(core, bias, queries, grad_out, kv0, kv1, kv2):
    wide = GROUP * HEAD_DIM

    def head(i, core_ref):
        return (2 - 2 * core_ref[0] + i) % KV_HEADS

    rows = pl.BlockSpec((LAYERS, TOK, wide), lambda i, c: (0, 0, head(i, c)))
    held = pl.BlockSpec(memory_space=pltpu.VMEM)
    theirs = pl.BlockSpec((3 * TOK, PAIR), lambda i, c: (0, jnp.minimum(i, 1)))
    mine = pl.BlockSpec((3 * TOK, PAIR), lambda i, c: (0, jnp.maximum(i - 2, 0)))
    return pl.pallas_call(
        attention_kernel,
        grid_spec=pltpu.PrefetchScalarGridSpec(
            num_scalar_prefetch=1,
            grid=(KV_HEADS,),
            in_specs=[held, rows, rows, held, held, held],
            out_specs=[rows, theirs, mine],
        ),
        out_shape=[
            jax.ShapeDtypeStruct(queries.shape, jnp.bfloat16),
            jax.ShapeDtypeStruct((3 * TOK, 2 * PAIR), jnp.bfloat16),
            jax.ShapeDtypeStruct((3 * TOK, 2 * PAIR), jnp.float32),
        ],
        compiler_params=pltpu.CompilerParams(vmem_limit_bytes=VMEM),
        cost_estimate=pl.CostEstimate(flops=6_000_000_000, bytes_accessed=9_000_000, transcendentals=1_400_000),
        name="attention",
    )(core[None], bias, queries, grad_out, kv0, kv1, kv2)


def product_kernel(at_ref, own_ref, other_ref, *refs):
    block_refs, out_refs, acc_ref = refs[:4], refs[4:8], refs[8]
    zl, x, y = at_ref[0], at_ref[1], at_ref[2]
    right = jnp.concatenate([ref[...] for ref in block_refs], axis=0)
    for place in range(4):
        left = []
        for by in range(4):
            seq = (zl - by + 4) % 4
            left += [own_ref[place, seq], other_ref[place, seq]]
        acc_ref[place] = jnp.dot(jnp.concatenate(left, axis=1), right, preferred_element_type=jnp.float32)
    for by in range(4):
        start = pl.multiple_of((x + by) % 4 * 80, 16)
        for place in range(4):
            out_refs[by][(y - place + 4) % 4] = acc_ref[place, pl.ds(start, 80)].astype(jnp.bfloat16)


def products(at, own, other, blocks):
    held = pl.BlockSpec(memory_space=pltpu.VMEM)
    return pl.pallas_call(
        product_kernel,
        in_specs=[pl.BlockSpec(memory_space=pltpu.SMEM)] + [held] * 6,
        out_specs=[held] * 4,
        out_shape=[jax.ShapeDtypeStruct((4, 80, PAIR), jnp.bfloat16)] * 4,
        scratch_shapes=[pltpu.VMEM((4, WIDE, PAIR), jnp.float32)],
        compiler_params=pltpu.CompilerParams(vmem_limit_bytes=16 * 1024 * 1024),
        cost_estimate=pl.CostEstimate(flops=700_000_000, bytes_accessed=4_000_000, transcendentals=0),
        name="products",
    )(at, own, other, *blocks)


def mask_bias(position, ends):
    own = jnp.arange(TOK, dtype=jnp.int32)

    def doc(pos):
        return jnp.sum((pos[:, None] >= ends[None, :]).astype(jnp.int32), axis=1)

    query_doc = doc(position + own)
    zero, one, two = ((position - back * TOK + own) for back in (0, 1, 2))
    lower = own[:, None] <= own[None, :]
    seen = [(pos >= 0)[:, None] & (doc(pos)[:, None] == query_doc[None, :]) for pos in (zero, one, two)]
    seen = jnp.concatenate([jnp.where(lower, seen[0], seen[2]), seen[1]], axis=0)
    return jnp.where(seen, 0.0, -jnp.inf).astype(jnp.float32)


def pick(value, index, axis):
    return lax.dynamic_index_in_dim(value, index, axis, keepdims=False)


def total(parts):
    acc = parts[0].astype(jnp.float32)
    for part in parts[1:]:
        acc = acc + part.astype(jnp.float32)
    return acc


def on_device(queries, keys_values, grad_out, hidden_kv, doc_lengths):
    core, zh, x, y, zl = (lax.axis_index(name) for name in ("core", "zh", "x", "y", "zl"))
    first = core == 0
    position = ((x * 2 + zh) * 2 + core) * TOK
    kv = keys_values[0]
    half = KV_HEADS * HEAD_DIM
    kv2 = ctx_shift(kv, 2)
    kv1 = shift(jnp.where(first, kv, kv2), "core", 1)

    bias = mask_bias(position, jnp.cumsum(doc_lengths[0]))
    hidden = hidden_kv.transpose(0, 2, 1).reshape(4, 4, WIDE, TOK)
    states = [pick(hidden, y, 1)] + [shift(pick(hidden, (y + by) % 4, 1), "y", by) for by in (1, 2, 3)]

    dq, theirs, mine = attention(core, bias, queries[:, 0], grad_out[:, 0], kv, kv1, kv2)
    states, theirs = lax.optimization_barrier((states, theirs))
    theirs = shift(theirs, "core", 1)
    def terms(cols):
        mine_terms = mine[:, cols].reshape(3, TOK, PAIR)
        got_terms = theirs[:, cols].reshape(3, TOK, PAIR).astype(jnp.float32)
        return mine_terms, got_terms

    cameback = []
    parts = [slice(0, PAIR), slice(PAIR, 2 * PAIR)]
    for cols in parts:
        (_, m_one, m_two), (_, g_one, g_two) = terms(cols)
        back = jnp.concatenate([m_two + jnp.where(first, 0.0, g_one), g_two + jnp.where(first, m_one, 0.0)], axis=0)
        back = back.astype(jnp.bfloat16)
        cameback.append(ctx_shift(back, -2))

    mine, theirs, _ = lax.optimization_barrier((mine, theirs, back))
    halves = []
    for cols, came in zip(parts, cameback):
        (m_own, m_one, _), (g_own, g_one, _) = terms(cols)
        here = jnp.concatenate([m_own + jnp.where(first, g_one, 0.0), g_own + jnp.where(first, 0.0, m_one)], axis=0)
        halves.append((here, came))
    states, _ = lax.optimization_barrier((states, here))
    states = jnp.stack(states)
    other_states = shift(states, "core", 1)

    blocks, reduced = [], []
    for here, came in halves:
        block = (here + came.astype(jnp.float32)).astype(jnp.bfloat16)
        blocks.append(block)
        gathered = [block] + [shift(block, "zl", by) for by in (1, 2, 3)]
        pieces = products(jnp.stack([zl, x, y]).astype(jnp.int32), states, other_states, gathered)
        got = [pieces[0]] + [shift(pieces[by], "x", by) for by in (1, 2, 3)]
        reduced.append(total(got).astype(jnp.bfloat16))
    block = jnp.concatenate(blocks, axis=1)
    partial = []
    for part in reduced:
        got = [pick(part, y, 0)] + [shift(pick(part, (y + by) % 4, 0), "y", by) for by in (1, 2, 3)]
        partial.append(total(got).astype(jnp.bfloat16))
    partial = jnp.concatenate(partial, axis=1).reshape(2, 40, 2 * PAIR)
    rows = total([pick(partial, zh, 0), shift(pick(partial, 1 - zh, 0), "zh", 1)]).reshape(2, 20, 2 * PAIR)
    def assemble(own, other):
        count = own.shape[0]
        cols = jnp.concatenate([jnp.where(first, own, other), jnp.where(first, other, own)], axis=1)
        return cols.reshape(count, KV_HEADS, 2, HEAD_DIM).transpose(0, 2, 1, 3).reshape(count, KV_HEADS * PAIR)

    kv_out = assemble(block[:TOK], shift(block[TOK:], "core", 1))
    rows, kv_out = lax.optimization_barrier((rows, kv_out))
    ours = pick(rows, core, 0)
    others = shift(pick(rows, 1 - core, 0), "core", 1)
    low, high = jnp.where(first, ours, others), jnp.where(first, others, ours)
    heads = [part[:, i * HEAD_DIM : (i + 1) * HEAD_DIM] for part in (low, high) for i in range(4)]
    weight = jnp.concatenate(heads[0::2] + heads[1::2], axis=1)
    return dq[:, None], kv_out[None], weight


def solution(mesh):
    fine = Mesh(mesh.devices.reshape(4, 4, 4, 2, 2), AXES)
    dp, ctx = ("zl", "y"), ("x", "zh", "core")
    placed = (
        P(None, dp, ctx, None),
        P(dp, ctx, None),
        P(None, dp, ctx, None),
        P(None, ctx, dp),
        P(dp, None),
    )
    return jax.shard_map(
        on_device,
        mesh=fine,
        in_specs=placed,
        out_specs=(P(None, dp, ctx, None), P(dp, ctx, None), P(dp + ctx, None)),
        check_vma=False,
    )
```

```python
import functools
import math

import jax
import jax.numpy as jnp
from jax import lax
from jax.experimental import pallas as pl
from jax.experimental.pallas import tpu as pltpu
from jax.sharding import Mesh, PartitionSpec as P

KV_HEADS = 4
GROUP = 5
HEAD_DIM = 128
LAYERS = 2
TOK = 128
WIDE = 320
VMEM = 60 * 1024 * 1024
PAIR = 2 * HEAD_DIM
FACTOR = 1.0 / math.sqrt(HEAD_DIM)
AXES = ("zl", "y", "x", "zh", "core")
SIZES = {"zl": 4, "y": 4, "x": 4, "zh": 2, "core": 2}


def shift(value, axis, by):
    size = SIZES[axis]
    return lax.ppermute(value, axis, [(i, (i + by) % size) for i in range(size)])


def ctx_shift(value, by):
    pairs = [(i, i + by) for i in range(16) if 0 <= i + by < 16]
    return lax.ppermute(value, ("x", "zh", "core"), pairs)


def softmax_grad(s, dp, bias, lower, lower_b, upper_b):
    scale = FACTOR * math.log2(math.e)
    s0 = jnp.where(lower, s[:TOK], s[2 * TOK :]) * scale + bias[:TOK]
    s1 = s[TOK : 2 * TOK] * scale + bias[TOK:]
    top = jnp.max(jnp.maximum(s0, s1), axis=0, keepdims=True)
    e0, e1 = jnp.exp2(s0 - top), jnp.exp2(s1 - top)
    inv = 1.0 / jnp.sum(e0 + e1, axis=0, keepdims=True)
    p0, p1 = e0 * inv, e1 * inv
    d0 = p0 * jnp.where(lower, dp[:TOK], dp[2 * TOK :])
    d1 = p1 * dp[TOK : 2 * TOK]
    delta = jnp.sum(d0 + d1, axis=0, keepdims=True)
    d0, d1 = (d0 - p0 * delta).astype(jnp.bfloat16), (d1 - p1 * delta).astype(jnp.bfloat16)
    p0, p1 = p0.astype(jnp.bfloat16), p1.astype(jnp.bfloat16)
    p = jnp.concatenate([p0 * lower_b, p1, p0 * upper_b], axis=0)
    ds = jnp.concatenate([d0 * lower_b, d1, d0 * upper_b], axis=0)
    return p, ds


def attention_kernel(core_ref, bias_ref, q_ref, do_ref, kv0_ref, kv1_ref, kv2_ref, dq_ref, theirs_ref, mine_ref):
    head = (2 - 2 * core_ref[0] + pl.program_id(0)) % KV_HEADS
    key_cols = pl.ds(pl.multiple_of(head * HEAD_DIM, HEAD_DIM), HEAD_DIM)
    value_cols = pl.ds(pl.multiple_of((KV_HEADS + head) * HEAD_DIM, HEAD_DIM), HEAD_DIM)
    keys = jnp.concatenate([ref[:, key_cols] for ref in (kv0_ref, kv1_ref, kv2_ref)], axis=0)
    values = jnp.concatenate([ref[:, value_cols] for ref in (kv0_ref, kv1_ref, kv2_ref)], axis=0)
    keys_t = keys.T
    bias = bias_ref[...]
    key_at = lax.broadcasted_iota(jnp.int32, (TOK, TOK), 0)
    query_at = lax.broadcasted_iota(jnp.int32, (TOK, TOK), 1)
    lower = key_at <= query_at
    lower_b = lower.astype(jnp.float32).astype(jnp.bfloat16)
    upper_b = 1 - lower_b
    nt = (((1,), (1,)), ((), ()))

    def load(g):
        cols = slice(g * HEAD_DIM, (g + 1) * HEAD_DIM)
        q = jnp.concatenate([q_ref[0, :, cols], q_ref[1, :, cols]], axis=0)
        do = jnp.concatenate([do_ref[0, :, cols], do_ref[1, :, cols]], axis=0)
        s = lax.dot_general(keys, q, nt, preferred_element_type=jnp.float32)
        dp = lax.dot_general(values, do, nt, preferred_element_type=jnp.float32)
        return q, do, s, dp

    def store(g, q, do, p, ds, dk, dv):
        cols = slice(g * HEAD_DIM, (g + 1) * HEAD_DIM)
        dv += jnp.dot(p, do, preferred_element_type=jnp.float32)
        dk += jnp.dot(ds, q, preferred_element_type=jnp.float32)
        dq = jnp.dot(keys_t, ds, preferred_element_type=jnp.float32) * FACTOR
        dq = dq.astype(jnp.bfloat16).T
        dq_ref[0, :, cols] = dq[:TOK]
        dq_ref[1, :, cols] = dq[TOK:]
        return dk, dv

    dk = jnp.zeros((3 * TOK, HEAD_DIM), jnp.float32)
    dv = jnp.zeros((3 * TOK, HEAD_DIM), jnp.float32)
    following, done = load(0), None
    for g in range(GROUP):
        q, do, s, dp = following
        if g + 1 < GROUP:
            following = load(g + 1)
        if done is not None:
            dk, dv = store(*done, dk, dv)
        tiles = [slice(layer * TOK, (layer + 1) * TOK) for layer in range(LAYERS)]
        parts = [softmax_grad(s[:, t], dp[:, t], bias, lower, lower_b, upper_b) for t in tiles]
        p = jnp.concatenate([part[0] for part in parts], axis=1)
        ds = jnp.concatenate([part[1] for part in parts], axis=1)
        done = (g, q, do, p, ds)
    dk, dv = store(*done, dk, dv)
    both = jnp.concatenate([dk * FACTOR, dv], axis=1)

    @pl.when(pl.program_id(0) < 2)
    def _():
        theirs_ref[...] = both.astype(jnp.bfloat16)

    @pl.when(pl.program_id(0) >= 2)
    def _():
        mine_ref[...] = both


def attention(core, bias, queries, grad_out, kv0, kv1, kv2):
    wide = GROUP * HEAD_DIM

    def head(i, core_ref):
        return (2 - 2 * core_ref[0] + i) % KV_HEADS

    rows = pl.BlockSpec((LAYERS, TOK, wide), lambda i, c: (0, 0, head(i, c)))
    held = pl.BlockSpec(memory_space=pltpu.VMEM)
    theirs = pl.BlockSpec((3 * TOK, PAIR), lambda i, c: (0, jnp.minimum(i, 1)))
    mine = pl.BlockSpec((3 * TOK, PAIR), lambda i, c: (0, jnp.maximum(i - 2, 0)))
    return pl.pallas_call(
        attention_kernel,
        grid_spec=pltpu.PrefetchScalarGridSpec(
            num_scalar_prefetch=1,
            grid=(KV_HEADS,),
            in_specs=[held, rows, rows, held, held, held],
            out_specs=[rows, theirs, mine],
        ),
        out_shape=[
            jax.ShapeDtypeStruct(queries.shape, jnp.bfloat16),
            jax.ShapeDtypeStruct((3 * TOK, 2 * PAIR), jnp.bfloat16),
            jax.ShapeDtypeStruct((3 * TOK, 2 * PAIR), jnp.float32),
        ],
        compiler_params=pltpu.CompilerParams(vmem_limit_bytes=VMEM),
        cost_estimate=pl.CostEstimate(flops=6_000_000_000, bytes_accessed=9_000_000, transcendentals=1_400_000),
        name="attention",
    )(core[None], bias, queries, grad_out, kv0, kv1, kv2)


def product_kernel(at_ref, own_ref, other_ref, *refs):
    block_refs, out_refs, acc_ref = refs[:4], refs[4:8], refs[8]
    zl, x, y = at_ref[0], at_ref[1], at_ref[2]
    right = jnp.concatenate([ref[...] for ref in block_refs], axis=0)
    for place in range(4):
        left = []
        for by in range(4):
            seq = (zl - by + 4) % 4
            left += [own_ref[place, seq], other_ref[place, seq]]
        acc_ref[place] = jnp.dot(jnp.concatenate(left, axis=1), right, preferred_element_type=jnp.float32)
    for by in range(4):
        start = pl.multiple_of((x + by) % 4 * 80, 16)
        for place in range(4):
            out_refs[by][(y - place + 4) % 4] = acc_ref[place, pl.ds(start, 80)].astype(jnp.bfloat16)


def products(at, own, other, blocks):
    held = pl.BlockSpec(memory_space=pltpu.VMEM)
    return pl.pallas_call(
        product_kernel,
        in_specs=[pl.BlockSpec(memory_space=pltpu.SMEM)] + [held] * 6,
        out_specs=[held] * 4,
        out_shape=[jax.ShapeDtypeStruct((4, 80, PAIR), jnp.bfloat16)] * 4,
        scratch_shapes=[pltpu.VMEM((4, WIDE, PAIR), jnp.float32)],
        compiler_params=pltpu.CompilerParams(vmem_limit_bytes=16 * 1024 * 1024),
        cost_estimate=pl.CostEstimate(flops=700_000_000, bytes_accessed=4_000_000, transcendentals=0),
        name="products",
    )(at, own, other, *blocks)


def mask_bias(position, ends):
    own = jnp.arange(TOK, dtype=jnp.int32)

    def doc(pos):
        return jnp.sum((pos[:, None] >= ends[None, :]).astype(jnp.int32), axis=1)

    query_doc = doc(position + own)
    zero, one, two = ((position - back * TOK + own) for back in (0, 1, 2))
    lower = own[:, None] <= own[None, :]
    seen = [(pos >= 0)[:, None] & (doc(pos)[:, None] == query_doc[None, :]) for pos in (zero, one, two)]
    seen = jnp.concatenate([jnp.where(lower, seen[0], seen[2]), seen[1]], axis=0)
    return jnp.where(seen, 0.0, -jnp.inf).astype(jnp.float32)


def pick(value, index, axis):
    return lax.dynamic_index_in_dim(value, index, axis, keepdims=False)


def total(parts):
    acc = parts[0].astype(jnp.float32)
    for part in parts[1:]:
        acc = acc + part.astype(jnp.float32)
    return acc


def on_device(queries, keys_values, grad_out, hidden_kv, doc_lengths):
    core, zh, x, y, zl = (lax.axis_index(name) for name in ("core", "zh", "x", "y", "zl"))
    first = core == 0
    position = ((x * 2 + zh) * 2 + core) * TOK
    kv = keys_values[0]
    half = KV_HEADS * HEAD_DIM
    kv2 = ctx_shift(kv, 2)
    kv1 = shift(jnp.where(first, kv, kv2), "core", 1)

    bias = mask_bias(position, jnp.cumsum(doc_lengths[0]))
    hidden = hidden_kv.transpose(0, 2, 1).reshape(4, 4, WIDE, TOK)
    states = [pick(hidden, y, 1)] + [shift(pick(hidden, (y + by) % 4, 1), "y", by) for by in (1, 2, 3)]

    dq, theirs, mine = attention(core, bias, queries[:, 0], grad_out[:, 0], kv, kv1, kv2)
    states, theirs = lax.optimization_barrier((states, theirs))
    theirs = shift(theirs, "core", 1)
    def terms(cols):
        mine_terms = mine[:, cols].reshape(3, TOK, PAIR)
        got_terms = theirs[:, cols].reshape(3, TOK, PAIR).astype(jnp.float32)
        return mine_terms, got_terms

    cameback = []
    parts = [slice(0, PAIR), slice(PAIR, 2 * PAIR)]
    for cols in parts:
        (_, m_one, m_two), (_, g_one, g_two) = terms(cols)
        back = jnp.concatenate([m_two + jnp.where(first, 0.0, g_one), g_two + jnp.where(first, m_one, 0.0)], axis=0)
        back = back.astype(jnp.bfloat16)
        cameback.append(ctx_shift(back, -2))

    mine, theirs, _ = lax.optimization_barrier((mine, theirs, back))
    halves = []
    for cols, came in zip(parts, cameback):
        (m_own, m_one, _), (g_own, g_one, _) = terms(cols)
        here = jnp.concatenate([m_own + jnp.where(first, g_one, 0.0), g_own + jnp.where(first, 0.0, m_one)], axis=0)
        halves.append((here, came))
    states, _ = lax.optimization_barrier((states, here))
    states = jnp.stack(states)
    other_states = shift(states, "core", 1)

    blocks, reduced = [], []
    for here, came in halves:
        block = (here + came.astype(jnp.float32)).astype(jnp.bfloat16)
        blocks.append(block)
        two = shift(block, "zl", 2)
        gathered = [block, shift(block, "zl", 1), two, shift(block, "zl", 3)]
        pieces = products(jnp.stack([zl, x, y]).astype(jnp.int32), states, other_states, gathered)
        got = [pieces[0]] + [shift(pieces[by], "x", by) for by in (1, 2, 3)]
        reduced.append(total(got).astype(jnp.bfloat16))
    block = jnp.concatenate(blocks, axis=1)
    partial = []
    for part in reduced:
        got = [pick(part, y, 0)] + [shift(pick(part, (y + by) % 4, 0), "y", by) for by in (1, 2, 3)]
        partial.append(total(got).astype(jnp.bfloat16))
    partial = jnp.concatenate(partial, axis=1).reshape(2, 40, 2 * PAIR)
    rows = total([pick(partial, zh, 0), shift(pick(partial, 1 - zh, 0), "zh", 1)]).reshape(2, 20, 2 * PAIR)
    def assemble(own, other):
        count = own.shape[0]
        cols = jnp.concatenate([jnp.where(first, own, other), jnp.where(first, other, own)], axis=1)
        return cols.reshape(count, KV_HEADS, 2, HEAD_DIM).transpose(0, 2, 1, 3).reshape(count, KV_HEADS * PAIR)

    kv_out = assemble(block[:TOK], shift(block[TOK:], "core", 1))
    rows, kv_out = lax.optimization_barrier((rows, kv_out))
    ours = pick(rows, core, 0)
    others = shift(pick(rows, 1 - core, 0), "core", 1)
    low, high = jnp.where(first, ours, others), jnp.where(first, others, ours)
    heads = [part[:, i * HEAD_DIM : (i + 1) * HEAD_DIM] for part in (low, high) for i in range(4)]
    weight = jnp.concatenate(heads[0::2] + heads[1::2], axis=1)
    return dq[:, None], kv_out[None], weight


def solution(mesh):
    fine = Mesh(mesh.devices.reshape(4, 4, 4, 2, 2), AXES)
    dp, ctx = ("zl", "y"), ("x", "zh", "core")
    placed = (
        P(None, dp, ctx, None),
        P(dp, ctx, None),
        P(None, dp, ctx, None),
        P(None, ctx, dp),
        P(dp, None),
    )
    return jax.shard_map(
        on_device,
        mesh=fine,
        in_specs=placed,
        out_specs=(P(None, dp, ctx, None), P(dp, ctx, None), P(dp + ctx, None)),
        check_vma=False,
    )
```
